128 devices in a mesh: st: 16 (over x, z_lo, core), hr: 8 (over z_hi, y).
Axes of the slice: x: 4, y: 4, z: 4 (z_hi: 2, z_lo: 2; z = z_hi * 2 + z_lo), core: 2. Of those that a mesh axis runs over, the one named last changes fastest.
Arguments:
- cotangent: bfloat16 [256, 64, 4096], P('hr', None, 'st'), may hold values from -24 to 24
- field: bfloat16 [256, 64, 4096], P('hr', None, 'st'), may hold values from -1.5 to 1.5
- temporal: bfloat16 [256, 256], replicated, may hold values from -0.375 to 0.375
- embed: float32 [16, 4096], P(None, 'st'), may hold values from -5 to 5
Outputs:
- field_grad: bfloat16 [256, 64, 4096], P('hr', None, 'st')
- embed_grad: float32 [16, 4096], P(None, 'st')
The draws below stay inside these ranges and needn't reach their ends.
All inputs are finite; a program needn't handle non-finite values.
Results may differ from the reference program's by a relative error of at most 0.02.
Values may be sent and summed in bfloat16 or wider, within the bound.
A program may use at most 128 MiB of HBM per device.

```python
import math
import jax
import jax.numpy as jnp
from jax import lax

EMB = 16
CH = 64
T_SIZE = 256
NS = 4096


def draw_embed(key, part):
    group_key = jax.random.fold_in(key, 11)
    center_key = jax.random.fold_in(key, 12)
    offset_key = jax.random.fold_in(key, 13)
    station_order = jax.random.permutation(group_key, NS)
    cluster = station_order // 4
    centers = 2.5 * jax.random.normal(center_key, (EMB, NS // 4), jnp.float32)
    offsets = 0.5 * jax.random.normal(offset_key, (EMB, NS), jnp.float32)
    spread = jnp.take(centers, cluster, axis=1) + offsets
    return jnp.clip(spread, -5.0, 5.0)


def block_levels(stream_key, extent, cuts, low, top_value):
    def one(axis_at, parts):
        heights = jax.random.uniform(jax.random.fold_in(jax.random.fold_in(stream_key, 6), axis_at), (parts,), jnp.float32, low / len(cuts), top_value / len(cuts))
        return jnp.repeat(jnp.exp(heights), extent[axis_at] // parts).reshape((-1,) + (1,) * (len(extent) - axis_at - 1))

    loudness = one(*cuts[0])
    for cut in cuts[1:]:
        loudness = loudness * one(*cut)
    return loudness


def gaussian(key, shape, scale, most, split=(), kind=jnp.bfloat16):
    entries = scale * jax.random.normal(key, shape, jnp.float32)
    if split:
        entries = entries * block_levels(key, shape, split, -0.22, 0.18)
    return jnp.clip(entries, -most, most).astype(kind)


def setup_inputs(seed: int = 0) -> dict:
    key_list = jax.random.split(jax.random.key(seed), 5)
    cotangent = gaussian(key_list[0], (T_SIZE, CH, NS), 4.0, 24.0, ((0, 8), (2, 16)))
    field = gaussian(key_list[1], (T_SIZE, CH, NS), 0.25, 1.5, ((0, 8), (2, 16)))
    temporal = gaussian(key_list[2], (T_SIZE, T_SIZE), T_SIZE ** -0.5, 0.375)
    embed = draw_embed(jax.random.fold_in(key_list[4], 71), 0)
    return {"cotangent": cotangent, "field": field, "temporal": temporal, "embed": embed}


def reference(cotangent, field, temporal, embed):
    amplitude = 1.0 / math.sqrt(NS)
    cot_flat = cotangent.reshape(T_SIZE, CH * NS)
    mixed_cot = lax.dot_general(temporal, cot_flat, (((0,), (0,)), ((), ())), preferred_element_type=jnp.float32)
    mixed_cot = mixed_cot.astype(jnp.bfloat16).reshape(T_SIZE * CH, NS)
    sq_norm = lax.optimization_barrier(jnp.sum(embed * embed, axis=0))
    cross_term = jnp.dot(embed.T, embed, precision=lax.Precision.HIGHEST)
    distance = sq_norm[:, None] + sq_norm[None, :] - 2.0 * cross_term
    kernel = jnp.exp(distance * (-0.5 / EMB)) * amplitude
    kernel_bf = kernel.astype(jnp.bfloat16)
    field_grad = lax.dot_general(mixed_cot, kernel_bf, (((1,), (1,)), ((), ())), preferred_element_type=jnp.float32)
    field_grad = field_grad.astype(jnp.bfloat16).reshape(T_SIZE, CH, NS)
    gram = lax.dot_general(field.reshape(T_SIZE * CH, NS), mixed_cot, (((0,), (0,)), ((), ())), preferred_element_type=jnp.float32)
    weight = gram * kernel
    sym_weight = weight + weight.T
    embed_grad = jnp.dot(embed, sym_weight, precision=lax.Precision.HIGHEST) - embed * lax.optimization_barrier(jnp.sum(sym_weight, axis=0))[None, :]
    embed_grad = embed_grad * (1.0 / EMB)
    return (field_grad, embed_grad)
```

```python
import math

import jax
import jax.numpy as jnp
from jax import lax
from jax.experimental import pallas as pl
from jax.experimental.pallas import tpu as pltpu
from jax.sharding import PartitionSpec as P

F32 = jnp.float32
BF16 = jnp.bfloat16
MESH = pl.DeviceIdType.MESH
LOG2E = 1.0 / math.log(2.0)


def contract(a, b, dim_a, dim_b):
    return lax.dot_general(a, b, (((dim_a,), (dim_b,)), ((), ())), preferred_element_type=F32)


def split3(v):
    high = v.astype(BF16)
    rest = v - high.astype(F32)
    mid = rest.astype(BF16)
    low = (rest - mid.astype(F32)).astype(BF16)
    return high, mid, low


def one_hot_matrix(keep):
    row = lax.broadcasted_iota(jnp.int32, (256, 256), 0)
    col = lax.broadcasted_iota(jnp.int32, (256, 256), 1)
    return jnp.where(keep(row, col), 1.0, 0.0).astype(BF16)


def swap_rows():
    return one_hot_matrix(lambda r, c: ((r >> 4) == (c & 15)) & ((r & 15) == (c >> 4)))


def identity():
    return one_hot_matrix(lambda r, c: r == c)


def swap_leading(src, dst, perm):
    n_a, n_b, width = src.shape
    for b in range(0, n_b, 16):
        for a in range(0, n_a, 16):
            tile = src[a : a + 16, b : b + 16, :].reshape(256, width)
            moved = contract(perm, tile, 1, 0).astype(BF16)
            dst[b : b + 16, a : a + 16, :] = moved.reshape(16, 16, width)


def norm_rows(sq, left, amp_log2):
    parts = [p.astype(F32) for p in split3(sq * (-LOG2E / 32.0) + amp_log2)]
    row = lax.broadcasted_iota(jnp.int32, (16, sq.shape[1]), 0)
    own = 0 if left else 3
    ones = 3 - own
    out = jnp.where((row >= ones) & (row < ones + 3), 1.0, 0.0)
    for q in range(3):
        out = jnp.where(row == own + q, parts[q], out)
    return out.astype(BF16)


def features(e, left, amp_log2):
    sq = jnp.sum(e * e, axis=0, keepdims=True)
    zero = jnp.zeros(e.shape, BF16)
    if left:
        h, m, l = split3(e * (LOG2E / 16.0))
        rows = [h, h, h, norm_rows(sq, True, amp_log2), m, m, l, zero]
    else:
        h, m, l = split3(e)
        rows = [h, m, l, norm_rows(sq, False, 0.0), h, m, h, zero]
    return jnp.concatenate([r.astype(F32) for r in rows], axis=0).astype(BF16)


def kernel(
    cot, field, temporal, embed, grad, egrad,
    raw, fraw, sent, fsent, crecv, pair, tile, left, feat_l, feat_r,
    eall, tmix, osend, orecv, esend, erecv,
    in_sem, send_sem, recv_sem,
):
    st = lax.axis_index("st")
    hr = lax.axis_index("hr")
    core = lax.rem(st, 2)
    col = st // 2
    me = hr * 8 + col
    x, z, y = st // 4, (hr // 4) * 2 + lax.rem(col, 2), lax.rem(hr, 4)
    partner = (st + 1 - 2 * core, hr)

    def peer(k):
        px = lax.rem(x + lax.rem(k, 4), 4)
        py = lax.rem(y + lax.rem(k // 4, 4), 4)
        pz = lax.rem(z + k // 16, 4)
        return px * 2 + lax.rem(pz, 2), (pz // 2) * 4 + py

    def load(i, src, dst):
        return pltpu.make_async_copy(src, dst, in_sem.at[i])

    load(0, cot, raw).start()
    load(1, field, fraw).start()

    barrier = pltpu.get_barrier_semaphore()

    @pl.loop(1, 64)
    def _(k):
        c, h = peer(k)
        pl.semaphore_signal(barrier, inc=1, device_id=(c * 2 + core, h), device_id_type=MESH)

    @pl.loop(0, 8)
    def _(c):
        pl.semaphore_signal(barrier, inc=1, device_id=(c * 2 + 1 - core, hr), device_id_type=MESH)

    perm = swap_rows()
    load(0, cot, raw).wait()
    swap_leading(raw, sent, perm)
    pl.semaphore_wait(barrier, 71)

    def push(i, src, dst, device):
        pltpu.make_async_remote_copy(
            src_ref=src, dst_ref=dst, send_sem=send_sem.at[i], recv_sem=recv_sem.at[i],
            device_id=device, device_id_type=MESH,
        ).start()

    def keep(i, src, dst):
        pltpu.make_async_copy(src, dst, recv_sem.at[i]).start()

    def settle(sem, ref):
        pltpu.make_async_copy(ref, ref, sem).wait()

    @pl.loop(1, 8)
    def _(k):
        c = lax.rem(col + k, 8)
        push(0, embed, eall.at[0, col], (c * 2 + core, hr))

    @pl.loop(0, 8)
    def _(k):
        c = lax.rem(col + k, 8)
        push(0, embed, eall.at[1, col], (c * 2 + 1 - core, hr))

    keep(0, embed, eall.at[0, col])

    @pl.loop(1, 64)
    def _(k):
        c, h = peer(k)
        push(1, sent.at[h * 8 + c], crecv.at[col, hr], (c * 2 + core, h))

    keep(1, sent.at[me], crecv.at[col, hr])

    load(1, field, fraw).wait()
    swap_leading(fraw, fsent, perm)
    hours = pl.ds(pl.multiple_of(256 + hr * 32, 32), 32)

    @pl.loop(1, 64)
    def _(k):
        c, h = peer(k)
        push(2, fsent.at[h * 8 + c], pair.at[0, col, hours, :], (c * 2 + core, h))

    keep(2, fsent.at[me], pair.at[0, col, hours, :])

    eye = identity()
    tmix[...] = contract(eye, temporal[...], 1, 1).astype(BF16)
    amp_log2 = -0.5 * math.log2(4096.0)
    settle(recv_sem.at[0], eall)

    @pl.loop(0, 8)
    def _(a):
        e = eall[0, a]
        feat_l[a] = contract(eye, features(e, True, amp_log2), 1, 1).astype(BF16)
        feat_r[0, a] = features(e, False, 0.0)
        feat_r[1, a] = features(eall[1, a], False, 0.0)

    @pl.loop(0, 8)
    def _(a):
        rows = feat_l[a]
        for p in range(2):
            for b in range(8):
                tile[a, p, b] = jnp.exp2(contract(rows, feat_r[p, b], 1, 0)).astype(BF16)

    settle(recv_sem.at[1], crecv)

    @pl.loop(0, 8)
    def _(a):
        mixed = contract(tmix[...], crecv[a].reshape(256, 256), 1, 0).astype(BF16)
        pair[0, a, :256, :] = mixed
        push(3, pair.at[0, a, pl.ds(0, 256), :], pair.at[1, a, pl.ds(0, 256), :], partner)

    @pl.loop(0, 8, step=4)
    def _(a):
        for q in range(4):
            left[a + q, :, 256:] = contract(eye, pair[0, a + q, :256, :], 1, 1).astype(BF16)

    settle(recv_sem.at[3], pair.at[1, :, pl.ds(0, 256), :])

    def column(k):
        return lax.rem(x + k // 2, 4) * 2 + lax.rem(lax.rem(col, 2) + k, 2)

    def row(k):
        return lax.rem(hr // 4 + k // 4, 2) * 4 + lax.rem(y + k, 4)

    @pl.loop(0, 8)
    def _(k):
        a = column(k)
        acc = jnp.zeros((256, 256), F32)
        for p in range(2):
            for b in range(8):
                acc += contract(pair[p, b, :256, :], tile[a, p, b], 1, 1)
        osend[a] = acc.astype(BF16).reshape(8, 32, 256)

        @pl.loop(0, 8)
        def _(q):
            h = row(q)

            @pl.when(h * 8 + a != me)
            def _():
                push(4, osend.at[a, h], orecv.at[me], (a * 2 + core, h))

    keep(4, osend.at[col, hr], orecv.at[me])

    settle(recv_sem.at[2], pair.at[0, :, pl.ds(256, 256), :])
    push(5, pair.at[0, :, pl.ds(256, 256), :], pair.at[1, :, pl.ds(256, 256), :], partner)

    @pl.loop(0, 8, step=4)
    def _(a):
        for q in range(4):
            left[a + q, :, :256] = contract(eye, pair[0, a + q, 256:, :], 1, 1).astype(BF16)

    settle(recv_sem.at[5], pair.at[1, :, pl.ds(256, 256), :])

    @pl.loop(0, 8)
    def _(k):
        a = column(k)
        rows = left[a]
        for p in range(2):
            for b in range(8):
                tile[a, p, b] = contract(rows, pair[p, b], 1, 0).astype(BF16) * tile[a, p, b]
        acc = jnp.zeros((64, 256), F32)
        for p in range(2):
            for b in range(8):
                acc += contract(feat_r[p, b, :64, :], tile[a, p, b], 1, 1)
        part = acc[:16] + acc[16:32] + acc[32:48] - eall[0, a] * acc[48:49]
        esend[a] = (part * (1.0 / 16.0)).astype(BF16)

        @pl.loop(0, 8)
        def _(q):
            h = row(q)

            @pl.when(h * 8 + a != me)
            def _():
                push(6, esend.at[a], erecv.at[me], (a * 2 + core, h))

    keep(6, esend.at[col], erecv.at[me])

    settle(recv_sem.at[4], orecv)
    swap_leading(orecv, grad, perm)
    settle(recv_sem.at[6], erecv)
    egrad[...] = jnp.sum(erecv[...].astype(F32), axis=0)

    settle(send_sem.at[0], eall.at[0])
    settle(send_sem.at[0], eall.at[0, pl.ds(0, 7)])
    settle(send_sem.at[1], sent.at[pl.ds(0, 63)])
    settle(send_sem.at[2], sent.at[pl.ds(0, 63)])
    settle(send_sem.at[3], pair.at[1, :, pl.ds(0, 256), :])
    settle(send_sem.at[4], orecv.at[pl.ds(0, 63)])
    settle(send_sem.at[5], pair.at[1, :, pl.ds(256, 256), :])
    settle(send_sem.at[6], erecv.at[pl.ds(0, 63)])


def on_device(cot, field, temporal, embed):
    anywhere = pl.BlockSpec(memory_space=pl.ANY)
    vmem = pl.BlockSpec(memory_space=pltpu.VMEM)
    block = (64, 32, 256)
    return pl.pallas_call(
        kernel,
        out_shape=(
            jax.ShapeDtypeStruct((32, 64, 256), BF16),
            jax.ShapeDtypeStruct((16, 256), F32),
        ),
        in_specs=[anywhere, anywhere, vmem, vmem],
        out_specs=(vmem, vmem),
        scratch_shapes=[
            pltpu.VMEM((32, 64, 256), BF16),
            pltpu.VMEM((32, 64, 256), BF16),
            pltpu.VMEM(block, BF16),
            pltpu.VMEM(block, BF16),
            pltpu.VMEM((8, 8, 32, 256), BF16),
            pltpu.VMEM((2, 8, 512, 256), BF16),
            pltpu.VMEM((8, 2, 8, 256, 256), BF16),
            pltpu.VMEM((8, 256, 512), BF16),
            pltpu.VMEM((8, 256, 128), BF16),
            pltpu.VMEM((2, 8, 128, 256), BF16),
            pltpu.VMEM((2, 8, 16, 256), F32),
            pltpu.VMEM((256, 256), BF16),
            pltpu.VMEM((8, 8, 32, 256), BF16),
            pltpu.VMEM(block, BF16),
            pltpu.VMEM((8, 16, 256), BF16),
            pltpu.VMEM((64, 16, 256), BF16),
            pltpu.SemaphoreType.DMA((2,)),
            pltpu.SemaphoreType.DMA((7,)),
            pltpu.SemaphoreType.DMA((7,)),
        ],
        compiler_params=pltpu.CompilerParams(
            collective_id=0, has_side_effects=True, vmem_limit_bytes=50 * 2**20
        ),
    )(cot, field, temporal, embed)


def solution(mesh):
    return jax.shard_map(
        on_device,
        mesh=mesh,
        in_specs=(P("hr", None, "st"), P("hr", None, "st"), P(), P(None, "st")),
        out_specs=(P("hr", None, "st"), P(None, "st")),
        check_vma=False,
    )
```

```python
import math

import jax
import jax.numpy as jnp
from jax import lax
from jax.experimental import pallas as pl
from jax.experimental.pallas import tpu as pltpu
from jax.sharding import PartitionSpec as P

F32 = jnp.float32
BF16 = jnp.bfloat16
MESH = pl.DeviceIdType.MESH
LOG2E = 1.0 / math.log(2.0)


def contract(a, b, dim_a, dim_b):
    return lax.dot_general(a, b, (((dim_a,), (dim_b,)), ((), ())), preferred_element_type=F32)


def split3(v):
    high = v.astype(BF16)
    rest = v - high.astype(F32)
    mid = rest.astype(BF16)
    low = (rest - mid.astype(F32)).astype(BF16)
    return high, mid, low


def one_hot_matrix(keep):
    row = lax.broadcasted_iota(jnp.int32, (256, 256), 0)
    col = lax.broadcasted_iota(jnp.int32, (256, 256), 1)
    return jnp.where(keep(row, col), 1.0, 0.0).astype(BF16)


def swap_rows():
    return one_hot_matrix(lambda r, c: ((r >> 4) == (c & 15)) & ((r & 15) == (c >> 4)))


def identity():
    return one_hot_matrix(lambda r, c: r == c)


def swap_leading(src, dst, perm):
    n_a, n_b, width = src.shape
    for b in range(0, n_b, 16):
        for a in range(0, n_a, 16):
            tile = src[a : a + 16, b : b + 16, :].reshape(256, width)
            moved = contract(perm, tile, 1, 0).astype(BF16)
            dst[b : b + 16, a : a + 16, :] = moved.reshape(16, 16, width)


def norm_rows(sq, left, amp_log2):
    parts = [p.astype(F32) for p in split3(sq * (-LOG2E / 32.0) + amp_log2)]
    row = lax.broadcasted_iota(jnp.int32, (16, sq.shape[1]), 0)
    own = 0 if left else 3
    ones = 3 - own
    out = jnp.where((row >= ones) & (row < ones + 3), 1.0, 0.0)
    for q in range(3):
        out = jnp.where(row == own + q, parts[q], out)
    return out.astype(BF16)


def features(e, left, amp_log2):
    sq = jnp.sum(e * e, axis=0, keepdims=True)
    zero = jnp.zeros(e.shape, BF16)
    if left:
        h, m, l = split3(e * (LOG2E / 16.0))
        rows = [h, h, h, norm_rows(sq, True, amp_log2), m, m, l, zero]
    else:
        h, m, l = split3(e)
        rows = [h, m, l, norm_rows(sq, False, 0.0), h, m, h, zero]
    return jnp.concatenate(rows, axis=0)


def kernel(
    cot, field, temporal_in, embed_in, grad, egrad,
    raw, fraw, temporal, embed, sent, fsent, crecv, pair, tile, left, feat_l, feat_r,
    eall, tmix, osend, orecv, esend, erecv, gsend, grecv,
    in_sem, send_sem, recv_sem,
):
    st = lax.axis_index("st")
    hr = lax.axis_index("hr")
    core = lax.rem(st, 2)
    col = st // 2
    me = hr * 8 + col
    x, z, y = st // 4, (hr // 4) * 2 + lax.rem(col, 2), lax.rem(hr, 4)
    partner = (st + 1 - 2 * core, hr)

    def peer(k):
        step = lax.rem(k, 4)
        px = lax.rem(x + step, 4)
        py = lax.rem(y + k // 4 + step, 4)
        pz = lax.rem(z + k // 16 + step, 4)
        return px * 2 + lax.rem(pz, 2), (pz // 2) * 4 + py

    def load(i, src, dst):
        return pltpu.make_async_copy(src, dst, in_sem.at[i])

    load(2, embed_in, embed).start()
    load(0, cot, raw).start()
    load(3, temporal_in, temporal).start()
    load(1, field, fraw).start()

    barrier = pltpu.get_barrier_semaphore()

    @pl.loop(1, 64)
    def _(k):
        c, h = peer(k)
        pl.semaphore_signal(barrier, inc=1, device_id=(c * 2 + core, h), device_id_type=MESH)

    @pl.loop(0, 8)
    def _(c):
        pl.semaphore_signal(barrier, inc=1, device_id=(c * 2 + 1 - core, hr), device_id_type=MESH)

    perm = swap_rows()
    load(0, cot, raw).wait()
    swap_leading(raw, sent, perm)
    load(2, embed_in, embed).wait()
    pl.semaphore_wait(barrier, 71)

    def push(i, src, dst, device):
        pltpu.make_async_remote_copy(
            src_ref=src, dst_ref=dst, send_sem=send_sem.at[i], recv_sem=recv_sem.at[i],
            device_id=device, device_id_type=MESH,
        ).start()

    def keep(i, src, dst):
        pltpu.make_async_copy(src, dst, recv_sem.at[i]).start()

    def settle(sem, ref):
        pltpu.make_async_copy(ref, ref, sem).wait()

    @pl.loop(1, 8)
    def _(k):
        c = lax.rem(col + k, 8)
        push(0, embed, eall.at[0, col], (c * 2 + core, hr))

    @pl.loop(0, 8)
    def _(k):
        c = lax.rem(col + k, 8)
        push(0, embed, eall.at[1, col], (c * 2 + 1 - core, hr))

    keep(0, embed, eall.at[0, col])

    @pl.loop(1, 64)
    def _(k):
        c, h = peer(k)
        push(1, sent.at[h * 8 + c], crecv.at[col, hr], (c * 2 + core, h))

    keep(1, sent.at[me], crecv.at[col, hr])

    load(1, field, fraw).wait()
    swap_leading(fraw, fsent, perm)
    hours = pl.ds(pl.multiple_of(256 + hr * 32, 32), 32)

    def push_field(k):
        c, h = peer(k)
        push(2, fsent.at[h * 8 + c], pair.at[0, col, hours, :], (c * 2 + core, h))

    eye = identity()
    load(3, temporal_in, temporal).wait()
    tmix[...] = contract(eye, temporal[...], 1, 1).astype(BF16)
    amp_log2 = -0.5 * math.log2(4096.0)
    settle(recv_sem.at[0], eall)

    @pl.loop(0, 8, step=2)
    def _(a):
        for q in range(2):
            e = eall[0, a + q]
            feat_l[a + q] = contract(eye, features(e, True, amp_log2), 1, 1).astype(BF16)
            feat_r[0, a + q] = features(e, False, 0.0)
            feat_r[1, a + q] = features(eall[1, a + q], False, 0.0)

    def station_tiles(a, p):
        rows = feat_l[a]
        for b in range(8):
            tile[a, p, b] = jnp.exp2(contract(rows, feat_r[p, b], 1, 0)).astype(BF16)

    @pl.loop(0, 8)
    def _(a):
        @pl.when(a > 0)
        def _():
            push_field(a * 8)

        for q in range(1, 8):
            push_field(a * 8 + q)
        station_tiles(a, 0)

    keep(2, fsent.at[me], pair.at[0, col, hours, :])

    settle(recv_sem.at[1], crecv)

    @pl.loop(0, 8, step=2)
    def _(a):
        for q in range(2):
            mixed = contract(tmix[...], crecv[a + q].reshape(256, 256), 1, 0).astype(BF16)
            pair[0, a + q, :256, :] = mixed
        both = pl.ds(a, 2)
        push(3, pair.at[0, both, pl.ds(0, 256), :], pair.at[1, both, pl.ds(0, 256), :], partner)

    @pl.loop(0, 8)
    def _(a):
        left[a, :, 256:] = contract(eye, pair[0, a, :256, :], 1, 1).astype(BF16)
        station_tiles(a, 1)

    settle(recv_sem.at[3], pair.at[1, :, pl.ds(0, 256), :])

    def column(k):
        return lax.rem(x + k // 2, 4) * 2 + lax.rem(lax.rem(col, 2) + k, 2)

    def row(k):
        return lax.rem(hr // 4 + k // 4, 2) * 4 + lax.rem(y + k, 4)

    def grad_block(a):
        acc = jnp.zeros((256, 256), F32)
        for p in range(2):
            for b in range(8):
                acc += contract(pair[p, b, :256, :], tile[a, p, b], 1, 1)
        osend[a] = acc.astype(BF16).reshape(8, 32, 256)

    def push_grad(a, first):
        for q in range(first, 8):
            h = row(q)
            push(4, osend.at[a, h], orecv.at[me], (a * 2 + core, h))

    @pl.loop(1, 8)
    def _(k):
        a = column(k)
        grad_block(a)
        push_grad(a, 0)

    grad_block(col)
    push_grad(col, 1)
    keep(4, osend.at[col, hr], orecv.at[me])

    settle(recv_sem.at[2], pair.at[0, :, pl.ds(256, 256), :])
    push(5, pair.at[0, :, pl.ds(256, 256), :], pair.at[1, :, pl.ds(256, 256), :], partner)

    @pl.loop(0, 8, step=4)
    def _(a):
        for q in range(4):
            left[a + q, :, :256] = contract(eye, pair[0, a + q, 256:, :], 1, 1).astype(BF16)

    @pl.loop(0, 8)
    def _(a):
        rows = left[a]
        for d in range(5):
            b = lax.rem(a + d, 8)
            tile[a, 0, b] = contract(rows, pair[0, b], 1, 0).astype(BF16) * tile[a, 0, b]

    settle(recv_sem.at[5], pair.at[1, :, pl.ds(256, 256), :])

    @pl.loop(0, 8)
    def _(a):
        rows = left[a]
        for d in range(4):
            b = lax.rem(a + core + d, 8)
            tile[a, 1, b] = contract(rows, pair[1, b], 1, 0).astype(BF16) * tile[a, 1, b]

    def fold(acc, e):
        return acc[:16] + acc[16:32] + acc[32:48] - e * acc[48:49]

    @pl.loop(1, 9)
    def _(k):
        b = lax.rem(col + k, 8)
        acc = jnp.zeros((64, 256), F32)
        for d in range(4):
            a = lax.rem(b + 16 - core - d, 8)
            acc += contract(feat_r[0, a, :64, :], tile[a, 1, b], 1, 0)
        esend[1, b] = fold(acc, eall[1, b]).astype(BF16)
        push(6, esend.at[1, b], erecv.at[st], (b * 2 + 1 - core, hr))

    @pl.loop(1, 9)
    def _(k):
        a = lax.rem(col + k, 8)
        acc = jnp.zeros((64, 256), F32)
        for d in range(5):
            b = lax.rem(a + d, 8)
            acc += contract(feat_r[0, b, :64, :], tile[a, 0, b], 1, 1)
        for d in range(4):
            b = lax.rem(a + core + d, 8)
            acc += contract(feat_r[1, b, :64, :], tile[a, 1, b], 1, 1)
        for d in range(1, 4):
            b = lax.rem(a + 8 - d, 8)
            acc += contract(feat_r[0, b, :64, :], tile[b, 0, a], 1, 0)
        esend[0, a] = fold(acc, eall[0, a]).astype(BF16)

        @pl.when(k < 8)
        def _():
            push(6, esend.at[0, a], erecv.at[st], (a * 2 + core, hr))

    erecv[st] = esend[0, col]
    settle(recv_sem.at[6], erecv.at[pl.ds(0, 15)])
    gsend[...] = jnp.sum(erecv[...].astype(F32), axis=0) * (1.0 / 16.0)
    for k in range(1, 8):
        push(7, gsend, grecv.at[hr], (st, lax.rem(hr + k, 8)))
    grecv[hr] = gsend[...]

    settle(recv_sem.at[4], orecv)
    swap_leading(orecv, grad, perm)
    settle(recv_sem.at[7], grecv.at[pl.ds(0, 7)])
    egrad[...] = jnp.sum(grecv[...], axis=0)

    settle(send_sem.at[0], eall.at[0])
    settle(send_sem.at[0], eall.at[0, pl.ds(0, 7)])
    settle(send_sem.at[1], sent.at[pl.ds(0, 63)])
    settle(send_sem.at[2], sent.at[pl.ds(0, 63)])
    settle(send_sem.at[3], pair.at[1, :, pl.ds(0, 256), :])
    settle(send_sem.at[4], orecv.at[pl.ds(0, 63)])
    settle(send_sem.at[5], pair.at[1, :, pl.ds(256, 256), :])
    settle(send_sem.at[6], erecv.at[pl.ds(0, 15)])
    settle(send_sem.at[7], grecv.at[pl.ds(0, 7)])


def on_device(cot, field, temporal, embed):
    hbm = pl.BlockSpec(memory_space=pltpu.HBM)
    vmem = pl.BlockSpec(memory_space=pltpu.VMEM)
    block = (64, 32, 256)
    return pl.pallas_call(
        kernel,
        out_shape=(
            jax.ShapeDtypeStruct((32, 64, 256), BF16),
            jax.ShapeDtypeStruct((16, 256), F32),
        ),
        in_specs=[hbm, hbm, hbm, hbm],
        out_specs=(vmem, vmem),
        scratch_shapes=[
            pltpu.VMEM((32, 64, 256), BF16),
            pltpu.VMEM((32, 64, 256), BF16),
            pltpu.VMEM((256, 256), BF16),
            pltpu.VMEM((16, 256), F32),
            pltpu.VMEM(block, BF16),
            pltpu.VMEM(block, BF16),
            pltpu.VMEM((8, 8, 32, 256), BF16),
            pltpu.VMEM((2, 8, 512, 256), BF16),
            pltpu.VMEM((8, 2, 8, 256, 256), BF16),
            pltpu.VMEM((8, 256, 512), BF16),
            pltpu.VMEM((8, 256, 128), BF16),
            pltpu.VMEM((2, 8, 128, 256), BF16),
            pltpu.VMEM((2, 8, 16, 256), F32),
            pltpu.VMEM((256, 256), BF16),
            pltpu.VMEM((8, 8, 32, 256), BF16),
            pltpu.VMEM(block, BF16),
            pltpu.VMEM((2, 8, 16, 256), BF16),
            pltpu.VMEM((16, 16, 256), BF16),
            pltpu.VMEM((16, 256), F32),
            pltpu.VMEM((8, 16, 256), F32),
            pltpu.SemaphoreType.DMA((4,)),
            pltpu.SemaphoreType.DMA((8,)),
            pltpu.SemaphoreType.DMA((8,)),
        ],
        compiler_params=pltpu.CompilerParams(
            collective_id=0, has_side_effects=True, vmem_limit_bytes=52 * 2**20
        ),
    )(cot, field, temporal, embed)


def solution(mesh):
    return jax.shard_map(
        on_device,
        mesh=mesh,
        in_specs=(P("hr", None, "st"), P("hr", None, "st"), P(), P(None, "st")),
        out_specs=(P("hr", None, "st"), P(None, "st")),
        check_vma=False,
    )
```

```python
import math

import jax
import jax.numpy as jnp
from jax import lax
from jax.experimental import pallas as pl
from jax.experimental.pallas import tpu as pltpu
from jax.sharding import PartitionSpec as P

F32 = jnp.float32
BF16 = jnp.bfloat16
MESH = pl.DeviceIdType.MESH
LOG2E = 1.0 / math.log(2.0)


def contract(a, b, dim_a, dim_b):
    return lax.dot_general(a, b, (((dim_a,), (dim_b,)), ((), ())), preferred_element_type=F32)


def split3(v):
    high = v.astype(BF16)
    rest = v - high.astype(F32)
    mid = rest.astype(BF16)
    low = (rest - mid.astype(F32)).astype(BF16)
    return high, mid, low


def one_hot_matrix(keep):
    row = lax.broadcasted_iota(jnp.int32, (256, 256), 0)
    col = lax.broadcasted_iota(jnp.int32, (256, 256), 1)
    return jnp.where(keep(row, col), 1.0, 0.0).astype(BF16)


def swap_rows():
    return one_hot_matrix(lambda r, c: ((r >> 4) == (c & 15)) & ((r & 15) == (c >> 4)))


def identity():
    return one_hot_matrix(lambda r, c: r == c)


def swap_leading(src, dst, perm):
    n_a, n_b, width = src.shape
    for b in range(0, n_b, 16):
        for a in range(0, n_a, 16):
            tile = src[a : a + 16, b : b + 16, :].reshape(256, width)
            moved = contract(perm, tile, 1, 0).astype(BF16)
            dst[b : b + 16, a : a + 16, :] = moved.reshape(16, 16, width)


def norm_rows(sq, left, amp_log2):
    parts = [p.astype(F32) for p in split3(sq * (-LOG2E / 32.0) + amp_log2)]
    row = lax.broadcasted_iota(jnp.int32, (16, sq.shape[1]), 0)
    own = 0 if left else 3
    ones = 3 - own
    out = jnp.where((row >= ones) & (row < ones + 3), 1.0, 0.0)
    for q in range(3):
        out = jnp.where(row == own + q, parts[q], out)
    return out.astype(BF16)


def features(e, left, amp_log2):
    sq = jnp.sum(e * e, axis=0, keepdims=True)
    zero = jnp.zeros(e.shape, BF16)
    if left:
        h, m, l = split3(e * (LOG2E / 16.0))
        rows = [h, h, h, norm_rows(sq, True, amp_log2), m, m, l, zero]
    else:
        h, m, l = split3(e)
        rows = [h, m, l, norm_rows(sq, False, 0.0), h, m, h, zero]
    return jnp.concatenate(rows, axis=0)


def kernel(
    cot, field, temporal_in, embed_in, grad, egrad,
    raw, fraw, temporal, embed, sent, fsent, crecv, pair, tile, left, feat_l, feat_r,
    eall, tmix, osend, orecv, esend, erecv, gsend, grecv, inner, cross,
    in_sem, send_sem, recv_sem,
):
    st = lax.axis_index("st")
    hr = lax.axis_index("hr")
    core = lax.rem(st, 2)
    col = st // 2
    me = hr * 8 + col
    x, z, y = st // 4, (hr // 4) * 2 + lax.rem(col, 2), lax.rem(hr, 4)
    partner = (st + 1 - 2 * core, hr)

    def peer(k):
        step = lax.rem(k, 4)
        px = lax.rem(x + step, 4)
        py = lax.rem(y + k // 4 + step, 4)
        pz = lax.rem(z + k // 16 + step, 4)
        return px * 2 + lax.rem(pz, 2), (pz // 2) * 4 + py

    def load(i, src, dst):
        return pltpu.make_async_copy(src, dst, in_sem.at[i])

    load(2, embed_in, embed).start()
    load(0, cot, raw).start()
    load(3, temporal_in, temporal).start()
    load(1, field, fraw).start()

    barrier = pltpu.get_barrier_semaphore()

    @pl.loop(1, 64)
    def _(k):
        c, h = peer(k)
        pl.semaphore_signal(barrier, inc=1, device_id=(c * 2 + core, h), device_id_type=MESH)

    @pl.loop(0, 8)
    def _(c):
        pl.semaphore_signal(barrier, inc=1, device_id=(c * 2 + 1 - core, hr), device_id_type=MESH)

    perm = swap_rows()
    load(0, cot, raw).wait()
    swap_leading(raw, sent, perm)
    load(2, embed_in, embed).wait()
    pl.semaphore_wait(barrier, 71)

    def push(i, src, dst, device):
        pltpu.make_async_remote_copy(
            src_ref=src, dst_ref=dst, send_sem=send_sem.at[i], recv_sem=recv_sem.at[i],
            device_id=device, device_id_type=MESH,
        ).start()

    def keep(i, src, dst):
        pltpu.make_async_copy(src, dst, recv_sem.at[i]).start()

    def settle(sem, ref):
        pltpu.make_async_copy(ref, ref, sem).wait()

    @pl.loop(1, 8)
    def _(k):
        c = lax.rem(col + k, 8)
        push(0, embed, eall.at[0, col], (c * 2 + core, hr))

    @pl.loop(0, 8)
    def _(k):
        c = lax.rem(col + k, 8)
        push(0, embed, eall.at[1, col], (c * 2 + 1 - core, hr))

    keep(0, embed, eall.at[0, col])

    @pl.loop(1, 64)
    def _(k):
        c, h = peer(k)
        push(1, sent.at[h * 8 + c], crecv.at[col, hr], (c * 2 + core, h))

    keep(1, sent.at[me], crecv.at[col, hr])

    load(1, field, fraw).wait()
    swap_leading(fraw, fsent, perm)
    hours = pl.ds(pl.multiple_of(256 + hr * 32, 32), 32)

    def push_field(k):
        c, h = peer(k)
        push(2, fsent.at[h * 8 + c], pair.at[0, col, hours, :], (c * 2 + core, h))

    eye = identity()
    load(3, temporal_in, temporal).wait()
    tmix[...] = contract(eye, temporal[...], 1, 1).astype(BF16)
    amp_log2 = -0.5 * math.log2(4096.0)
    settle(recv_sem.at[0], eall)

    @pl.loop(0, 8, step=2)
    def _(a):
        for q in range(2):
            e = eall[0, a + q]
            feat_l[a + q] = contract(eye, features(e, True, amp_log2), 1, 1).astype(BF16)
            feat_r[0, a + q] = features(e, False, 0.0)
            feat_r[1, a + q] = features(eall[1, a + q], False, 0.0)

    def station_tiles(a, p):
        rows = feat_l[a]
        for b in range(8):
            tile[a, p, b] = jnp.exp2(contract(rows, feat_r[p, b], 1, 0)).astype(BF16)

    @pl.loop(0, 8)
    def _(a):
        @pl.when(a > 0)
        def _():
            push_field(a * 8)

        for q in range(1, 8):
            push_field(a * 8 + q)
        station_tiles(a, 0)
        station_tiles(a, 1)

    keep(2, fsent.at[me], pair.at[0, col, hours, :])

    settle(recv_sem.at[1], crecv)

    @pl.loop(0, 8, step=2)
    def _(a):
        for q in range(2):
            mixed = contract(tmix[...], crecv[a + q].reshape(256, 256), 1, 0).astype(BF16)
            pair[0, a + q, :256, :] = mixed
        both = pl.ds(a, 2)
        push(3, pair.at[0, both, pl.ds(0, 256), :], pair.at[1, both, pl.ds(0, 256), :], partner)

    @pl.loop(0, 8)
    def _(a):
        left[a, :, 256:] = contract(eye, pair[0, a, :256, :], 1, 1).astype(BF16)

    settle(recv_sem.at[3], pair.at[1, :, pl.ds(0, 256), :])

    def column(k):
        return lax.rem(x + k // 2, 4) * 2 + lax.rem(lax.rem(col, 2) + k, 2)

    def row(k):
        return lax.rem(hr // 4 + k // 4, 2) * 4 + lax.rem(y + k, 4)

    def grad_block(a):
        acc = jnp.zeros((256, 256), F32)
        for p in range(2):
            for b in range(8):
                acc += contract(pair[p, b, :256, :], tile[a, p, b], 1, 1)
        osend[a] = acc.astype(BF16).reshape(8, 32, 256)

    def push_grad(a, first):
        for q in range(first, 8):
            h = row(q)
            push(4, osend.at[a, h], orecv.at[me], (a * 2 + core, h))

    @pl.loop(1, 7, step=2)
    def _(k):
        grad_block(column(k))
        grad_block(column(k + 1))
        push_grad(column(k), 0)
        push_grad(column(k + 1), 0)

    grad_block(column(7))
    grad_block(col)
    push_grad(column(7), 0)
    push_grad(col, 1)
    keep(4, osend.at[col, hr], orecv.at[me])

    settle(recv_sem.at[2], pair.at[0, :, pl.ds(256, 256), :])
    push(5, pair.at[0, :, pl.ds(256, 256), :], pair.at[1, :, pl.ds(256, 256), :], partner)

    @pl.loop(0, 8, step=4)
    def _(a):
        for q in range(4):
            left[a + q, :, :256] = contract(eye, pair[0, a + q, 256:, :], 1, 1).astype(BF16)

    @pl.loop(0, 8, step=4)
    def _(first):
        for q in range(4):
            a = first + q
            rows = left[a]
            for d in range(5):
                b = lax.rem(a + d, 8)
                gram = contract(rows, pair[0, b], 1, 0).astype(BF16)
                inner[a, d] = gram * tile[a, 0, b]

    settle(recv_sem.at[5], pair.at[1, :, pl.ds(256, 256), :])

    @pl.loop(0, 8, step=4)
    def _(first):
        for q in range(4):
            a = first + q
            rows = left[a]
            for d in range(4):
                b = lax.rem(a + core + d, 8)
                gram = contract(rows, pair[1, b], 1, 0).astype(BF16)
                cross[a, d] = gram * tile[a, 1, b]

    def fold(acc, e):
        return acc[:16] + acc[16:32] + acc[32:48] - e * acc[48:49]

    def other_part(b):
        acc = jnp.zeros((64, 256), F32)
        for d in range(4):
            a = lax.rem(b + 16 - core - d, 8)
            acc += contract(feat_r[0, a, :64, :], cross[a, d], 1, 0)
        return fold(acc, eall[1, b]).astype(BF16)

    def own_part(a):
        acc = jnp.zeros((64, 256), F32)
        for d in range(5):
            acc += contract(feat_r[0, lax.rem(a + d, 8), :64, :], inner[a, d], 1, 1)
        for d in range(4):
            acc += contract(feat_r[1, lax.rem(a + core + d, 8), :64, :], cross[a, d], 1, 1)
        for d in range(1, 4):
            b = lax.rem(a + 8 - d, 8)
            acc += contract(feat_r[0, b, :64, :], inner[b, d], 1, 0)
        return fold(acc, eall[0, a]).astype(BF16)

    @pl.loop(1, 9, step=2)
    def _(k):
        for q in range(2):
            b = lax.rem(col + k + q, 8)
            esend[1, b] = other_part(b)
        for q in range(2):
            b = lax.rem(col + k + q, 8)
            push(6, esend.at[1, b], erecv.at[st], (b * 2 + 1 - core, hr))

    @pl.loop(1, 9, step=2)
    def _(k):
        for q in range(2):
            a = lax.rem(col + k + q, 8)
            esend[0, a] = own_part(a)
        for q in range(2):
            a = lax.rem(col + k + q, 8)

            @pl.when(k + q < 8)
            def _():
                push(6, esend.at[0, a], erecv.at[st], (a * 2 + core, hr))

    erecv[st] = esend[0, col]
    settle(recv_sem.at[6], erecv.at[pl.ds(0, 15)])
    gsend[...] = jnp.sum(erecv[...].astype(F32), axis=0) * (1.0 / 16.0)
    for k in range(1, 8):
        push(7, gsend, grecv.at[hr], (st, lax.rem(hr + k, 8)))
    grecv[hr] = gsend[...]

    settle(recv_sem.at[4], orecv)
    swap_leading(orecv, grad, perm)
    settle(recv_sem.at[7], grecv.at[pl.ds(0, 7)])
    egrad[...] = jnp.sum(grecv[...], axis=0)

    settle(send_sem.at[0], eall.at[0])
    settle(send_sem.at[0], eall.at[0, pl.ds(0, 7)])
    settle(send_sem.at[1], sent.at[pl.ds(0, 63)])
    settle(send_sem.at[2], sent.at[pl.ds(0, 63)])
    settle(send_sem.at[3], pair.at[1, :, pl.ds(0, 256), :])
    settle(send_sem.at[4], orecv.at[pl.ds(0, 63)])
    settle(send_sem.at[5], pair.at[1, :, pl.ds(256, 256), :])
    settle(send_sem.at[6], erecv.at[pl.ds(0, 15)])
    settle(send_sem.at[7], grecv.at[pl.ds(0, 7)])


def on_device(cot, field, temporal, embed):
    hbm = pl.BlockSpec(memory_space=pltpu.HBM)
    vmem = pl.BlockSpec(memory_space=pltpu.VMEM)
    block = (64, 32, 256)
    return pl.pallas_call(
        kernel,
        out_shape=(
            jax.ShapeDtypeStruct((32, 64, 256), BF16),
            jax.ShapeDtypeStruct((16, 256), F32),
        ),
        in_specs=[hbm, hbm, hbm, hbm],
        out_specs=(vmem, vmem),
        scratch_shapes=[
            pltpu.VMEM((32, 64, 256), BF16),
            pltpu.VMEM((32, 64, 256), BF16),
            pltpu.VMEM((256, 256), BF16),
            pltpu.VMEM((16, 256), F32),
            pltpu.VMEM(block, BF16),
            pltpu.VMEM(block, BF16),
            pltpu.VMEM((8, 8, 32, 256), BF16),
            pltpu.VMEM((2, 8, 512, 256), BF16),
            pltpu.VMEM((8, 2, 8, 256, 256), BF16),
            pltpu.VMEM((8, 256, 512), BF16),
            pltpu.VMEM((8, 256, 128), BF16),
            pltpu.VMEM((2, 8, 128, 256), BF16),
            pltpu.VMEM((2, 8, 16, 256), F32),
            pltpu.VMEM((256, 256), BF16),
            pltpu.VMEM((8, 8, 32, 256), BF16),
            pltpu.VMEM(block, BF16),
            pltpu.VMEM((2, 8, 16, 256), BF16),
            pltpu.VMEM((16, 16, 256), BF16),
            pltpu.VMEM((16, 256), F32),
            pltpu.VMEM((8, 16, 256), F32),
            pltpu.VMEM((8, 5, 256, 256), BF16),
            pltpu.VMEM((8, 4, 256, 256), BF16),
            pltpu.SemaphoreType.DMA((4,)),
            pltpu.SemaphoreType.DMA((8,)),
            pltpu.SemaphoreType.DMA((8,)),
        ],
        compiler_params=pltpu.CompilerParams(
            collective_id=0, has_side_effects=True, vmem_limit_bytes=52 * 2**20
        ),
    )(cot, field, temporal, embed)


def solution(mesh):
    return jax.shard_map(
        on_device,
        mesh=mesh,
        in_specs=(P("hr", None, "st"), P("hr", None, "st"), P(), P(None, "st")),
        out_specs=(P("hr", None, "st"), P(None, "st")),
        check_vma=False,
    )
```

```python
import math

import jax
import jax.numpy as jnp
from jax import lax
from jax.experimental import pallas as pl
from jax.experimental.pallas import tpu as pltpu
from jax.sharding import PartitionSpec as P

F32 = jnp.float32
BF16 = jnp.bfloat16
MESH = pl.DeviceIdType.MESH
LOG2E = 1.0 / math.log(2.0)


def contract(a, b, dim_a, dim_b):
    return lax.dot_general(a, b, (((dim_a,), (dim_b,)), ((), ())), preferred_element_type=F32)


def split3(v):
    high = v.astype(BF16)
    rest = v - high.astype(F32)
    mid = rest.astype(BF16)
    low = (rest - mid.astype(F32)).astype(BF16)
    return high, mid, low


def one_hot_matrix(keep):
    row = lax.broadcasted_iota(jnp.int32, (256, 256), 0)
    col = lax.broadcasted_iota(jnp.int32, (256, 256), 1)
    return jnp.where(keep(row, col), 1.0, 0.0).astype(BF16)


def swap_rows():
    return one_hot_matrix(lambda r, c: ((r >> 4) == (c & 15)) & ((r & 15) == (c >> 4)))


def identity():
    return one_hot_matrix(lambda r, c: r == c)


def swap_leading(src, dst, perm):
    n_a, n_b, width = src.shape
    for b in range(0, n_b, 16):
        for a in range(0, n_a, 16):
            tile = src[a : a + 16, b : b + 16, :].reshape(256, width)
            moved = contract(perm, tile, 1, 0).astype(BF16)
            dst[b : b + 16, a : a + 16, :] = moved.reshape(16, 16, width)


def norm_rows(sq, left, amp_log2):
    parts = [p.astype(F32) for p in split3(sq * (-LOG2E / 32.0) + amp_log2)]
    row = lax.broadcasted_iota(jnp.int32, (16, sq.shape[1]), 0)
    own = 0 if left else 3
    ones = 3 - own
    out = jnp.where((row >= ones) & (row < ones + 3), 1.0, 0.0)
    for q in range(3):
        out = jnp.where(row == own + q, parts[q], out)
    return out.astype(BF16)


def features(e, left, amp_log2):
    sq = jnp.sum(e * e, axis=0, keepdims=True)
    zero = jnp.zeros(e.shape, BF16)
    if left:
        h, m, l = split3(e * (LOG2E / 16.0))
        rows = [h, h, h, norm_rows(sq, True, amp_log2), m, m, l, zero]
    else:
        h, m, l = split3(e)
        rows = [h, m, l, norm_rows(sq, False, 0.0), h, m, h, zero]
    return jnp.concatenate(rows, axis=0)


def kernel(
    cot, field, temporal_in, embed_in, grad, egrad,
    raw, fraw, temporal, embed, sent, fsent, crecv, pair, tile, left, feat_l, feat_r,
    eall, tmix, osend, orecv, esend, erecv, gsend, grecv, inner, cross,
    in_sem, send_sem, recv_sem,
):
    st = lax.axis_index("st")
    hr = lax.axis_index("hr")
    core = lax.rem(st, 2)
    col = st // 2
    me = hr * 8 + col
    x, z, y = st // 4, (hr // 4) * 2 + lax.rem(col, 2), lax.rem(hr, 4)
    partner = (st + 1 - 2 * core, hr)

    def peer(k):
        step = lax.rem(k, 4)
        px = lax.rem(x + step, 4)
        py = lax.rem(y + k // 4 + step, 4)
        pz = lax.rem(z + k // 16 + step, 4)
        return px * 2 + lax.rem(pz, 2), (pz // 2) * 4 + py

    def load(i, src, dst):
        return pltpu.make_async_copy(src, dst, in_sem.at[i])

    load(2, embed_in, embed).start()
    load(0, cot, raw).start()
    load(3, temporal_in, temporal).start()
    load(1, field, fraw).start()

    barrier = pltpu.get_barrier_semaphore()

    @pl.loop(1, 64)
    def _(k):
        c, h = peer(k)
        pl.semaphore_signal(barrier, inc=1, device_id=(c * 2 + core, h), device_id_type=MESH)

    @pl.loop(0, 8)
    def _(c):
        pl.semaphore_signal(barrier, inc=1, device_id=(c * 2 + 1 - core, hr), device_id_type=MESH)

    perm = swap_rows()
    load(0, cot, raw).wait()
    swap_leading(raw, sent, perm)
    load(2, embed_in, embed).wait()
    pl.semaphore_wait(barrier, 71)

    def push(i, src, dst, device):
        pltpu.make_async_remote_copy(
            src_ref=src, dst_ref=dst, send_sem=send_sem.at[i], recv_sem=recv_sem.at[i],
            device_id=device, device_id_type=MESH,
        ).start()

    def keep(i, src, dst):
        pltpu.make_async_copy(src, dst, recv_sem.at[i]).start()

    def settle(sem, ref):
        pltpu.make_async_copy(ref, ref, sem).wait()

    @pl.loop(1, 8)
    def _(k):
        c = lax.rem(col + k, 8)
        push(0, embed, eall.at[0, col], (c * 2 + core, hr))

    keep(0, embed, eall.at[0, col])

    @pl.loop(1, 64)
    def _(k):
        c, h = peer(k)
        push(1, sent.at[h * 8 + c], crecv.at[col, hr], (c * 2 + core, h))

    keep(1, sent.at[me], crecv.at[col, hr])

    load(1, field, fraw).wait()
    swap_leading(fraw, fsent, perm)
    hours = pl.ds(pl.multiple_of(256 + hr * 32, 32), 32)

    def push_field(k):
        c, h = peer(k)
        push(2, fsent.at[h * 8 + c], pair.at[0, col, hours, :], (c * 2 + core, h))

    eye = identity()
    load(3, temporal_in, temporal).wait()
    tmix[...] = contract(eye, temporal[...], 1, 1).astype(BF16)
    amp_log2 = -0.5 * math.log2(4096.0)
    settle(recv_sem.at[0], eall.at[0])
    push(8, eall.at[0], eall.at[1], partner)

    @pl.loop(0, 8, step=2)
    def _(a):
        for q in range(2):
            e = eall[0, a + q]
            feat_l[a + q] = contract(eye, features(e, True, amp_log2), 1, 1).astype(BF16)
            feat_r[0, a + q] = features(e, False, 0.0)

    def station_tiles(a, p):
        rows = feat_l[a]
        for b in range(8):
            tile[a, p, b] = jnp.exp2(contract(rows, feat_r[p, b], 1, 0)).astype(BF16)

    @pl.loop(0, 8)
    def _(a):
        @pl.when(a > 0)
        def _():
            push_field(a * 4)

        for q in range(1, 4):
            push_field(a * 4 + q)
        station_tiles(a, 0)

    settle(recv_sem.at[8], eall.at[1])

    @pl.loop(0, 8, step=2)
    def _(a):
        for q in range(2):
            feat_r[1, a + q] = features(eall[1, a + q], False, 0.0)

    @pl.loop(0, 8)
    def _(a):
        for q in range(4):
            push_field(32 + a * 4 + q)
        station_tiles(a, 1)

    keep(2, fsent.at[me], pair.at[0, col, hours, :])

    settle(recv_sem.at[1], crecv)

    @pl.loop(0, 8, step=2)
    def _(a):
        for q in range(2):
            mixed = contract(tmix[...], crecv[a + q].reshape(256, 256), 1, 0).astype(BF16)
            pair[0, a + q, :256, :] = mixed
        both = pl.ds(a, 2)
        push(3, pair.at[0, both, pl.ds(0, 256), :], pair.at[1, both, pl.ds(0, 256), :], partner)

    @pl.loop(0, 8)
    def _(a):
        left[a, :, 256:] = contract(eye, pair[0, a, :256, :], 1, 1).astype(BF16)

    settle(recv_sem.at[3], pair.at[1, :, pl.ds(0, 256), :])

    def column(k):
        return lax.rem(x + k // 2, 4) * 2 + lax.rem(lax.rem(col, 2) + k, 2)

    def row(k):
        return lax.rem(hr // 4 + k // 4, 2) * 4 + lax.rem(y + k, 4)

    def grad_block(a):
        acc = jnp.zeros((256, 256), F32)
        for p in range(2):
            for b in range(8):
                acc += contract(pair[p, b, :256, :], tile[a, p, b], 1, 1)
        osend[a] = acc.astype(BF16).reshape(8, 32, 256)

    def push_grad(a, first):
        for q in range(first, 8):
            h = row(q)
            push(4, osend.at[a, h], orecv.at[me], (a * 2 + core, h))

    @pl.loop(1, 7, step=2)
    def _(k):
        grad_block(column(k))
        grad_block(column(k + 1))
        push_grad(column(k), 0)
        push_grad(column(k + 1), 0)

    grad_block(column(7))
    grad_block(col)
    push_grad(column(7), 0)
    push_grad(col, 1)
    keep(4, osend.at[col, hr], orecv.at[me])

    settle(recv_sem.at[2], pair.at[0, :, pl.ds(256, 256), :])
    push(5, pair.at[0, :, pl.ds(256, 256), :], pair.at[1, :, pl.ds(256, 256), :], partner)

    @pl.loop(0, 8, step=4)
    def _(first):
        for q in range(4):
            a = first + q
            left[a, :, :256] = pair[0, a, 256:, :].T
            rows = left[a]
            for d in range(5):
                b = lax.rem(a + d, 8)
                gram = contract(rows, pair[0, b], 1, 0).astype(BF16)
                inner[a, d] = gram * tile[a, 0, b]

    settle(recv_sem.at[5], pair.at[1, :, pl.ds(256, 256), :])

    @pl.loop(0, 8, step=4)
    def _(first):
        for q in range(4):
            a = first + q
            rows = left[a]
            for d in range(4):
                b = lax.rem(a + core + d, 8)
                gram = contract(rows, pair[1, b], 1, 0).astype(BF16)
                cross[a, d] = gram * tile[a, 1, b]

    def fold(acc, e):
        return acc[:16] + acc[16:32] + acc[32:48] - e * acc[48:49]

    def other_part(b):
        acc = jnp.zeros((64, 256), F32)
        for d in range(4):
            a = lax.rem(b + 16 - core - d, 8)
            acc += contract(feat_r[0, a, :64, :], cross[a, d], 1, 0)
        return fold(acc, eall[1, b]).astype(BF16)

    def own_part(a):
        acc = jnp.zeros((64, 256), F32)
        for d in range(5):
            acc += contract(feat_r[0, lax.rem(a + d, 8), :64, :], inner[a, d], 1, 1)
        for d in range(4):
            acc += contract(feat_r[1, lax.rem(a + core + d, 8), :64, :], cross[a, d], 1, 1)
        for d in range(1, 4):
            b = lax.rem(a + 8 - d, 8)
            acc += contract(feat_r[0, b, :64, :], inner[b, d], 1, 0)
        return fold(acc, eall[0, a]).astype(BF16)

    @pl.loop(1, 9, step=2)
    def _(k):
        for q in range(2):
            b = lax.rem(col + k + q, 8)
            esend[1, b] = other_part(b)
        for q in range(2):
            b = lax.rem(col + k + q, 8)
            push(6, esend.at[1, b], erecv.at[st], (b * 2 + 1 - core, hr))

    @pl.loop(1, 9, step=2)
    def _(k):
        for q in range(2):
            a = lax.rem(col + k + q, 8)
            esend[0, a] = own_part(a)
        for q in range(2):
            a = lax.rem(col + k + q, 8)

            @pl.when(k + q < 8)
            def _():
                push(6, esend.at[0, a], erecv.at[st], (a * 2 + core, hr))

    erecv[st] = esend[0, col]
    settle(recv_sem.at[6], erecv.at[pl.ds(0, 15)])
    gsend[...] = jnp.sum(erecv[...].astype(F32), axis=0) * (1.0 / 16.0)
    for k in range(1, 8):
        push(7, gsend, grecv.at[hr], (st, lax.rem(hr + k, 8)))
    grecv[hr] = gsend[...]

    settle(recv_sem.at[4], orecv)
    swap_leading(orecv, grad, perm)
    settle(recv_sem.at[7], grecv.at[pl.ds(0, 7)])
    egrad[...] = jnp.sum(grecv[...], axis=0)

    settle(send_sem.at[0], eall.at[0, pl.ds(0, 7)])
    settle(send_sem.at[8], eall.at[1])
    settle(send_sem.at[1], sent.at[pl.ds(0, 63)])
    settle(send_sem.at[2], sent.at[pl.ds(0, 63)])
    settle(send_sem.at[3], pair.at[1, :, pl.ds(0, 256), :])
    settle(send_sem.at[4], orecv.at[pl.ds(0, 63)])
    settle(send_sem.at[5], pair.at[1, :, pl.ds(256, 256), :])
    settle(send_sem.at[6], erecv.at[pl.ds(0, 15)])
    settle(send_sem.at[7], grecv.at[pl.ds(0, 7)])


def on_device(cot, field, temporal, embed):
    hbm = pl.BlockSpec(memory_space=pltpu.HBM)
    vmem = pl.BlockSpec(memory_space=pltpu.VMEM)
    block = (64, 32, 256)
    return pl.pallas_call(
        kernel,
        out_shape=(
            jax.ShapeDtypeStruct((32, 64, 256), BF16),
            jax.ShapeDtypeStruct((16, 256), F32),
        ),
        in_specs=[hbm, hbm, hbm, hbm],
        out_specs=(vmem, vmem),
        scratch_shapes=[
            pltpu.VMEM((32, 64, 256), BF16),
            pltpu.VMEM((32, 64, 256), BF16),
            pltpu.VMEM((256, 256), BF16),
            pltpu.VMEM((16, 256), F32),
            pltpu.VMEM(block, BF16),
            pltpu.VMEM(block, BF16),
            pltpu.VMEM((8, 8, 32, 256), BF16),
            pltpu.VMEM((2, 8, 512, 256), BF16),
            pltpu.VMEM((8, 2, 8, 256, 256), BF16),
            pltpu.VMEM((8, 256, 512), BF16),
            pltpu.VMEM((8, 256, 128), BF16),
            pltpu.VMEM((2, 8, 128, 256), BF16),
            pltpu.VMEM((2, 8, 16, 256), F32),
            pltpu.VMEM((256, 256), BF16),
            pltpu.VMEM((8, 8, 32, 256), BF16),
            pltpu.VMEM(block, BF16),
            pltpu.VMEM((2, 8, 16, 256), BF16),
            pltpu.VMEM((16, 16, 256), BF16),
            pltpu.VMEM((16, 256), F32),
            pltpu.VMEM((8, 16, 256), F32),
            pltpu.VMEM((8, 5, 256, 256), BF16),
            pltpu.VMEM((8, 4, 256, 256), BF16),
            pltpu.SemaphoreType.DMA((4,)),
            pltpu.SemaphoreType.DMA((9,)),
            pltpu.SemaphoreType.DMA((9,)),
        ],
        compiler_params=pltpu.CompilerParams(
            collective_id=0, has_side_effects=True, vmem_limit_bytes=52 * 2**20
        ),
    )(cot, field, temporal, embed)


def solution(mesh):
    return jax.shard_map(
        on_device,
        mesh=mesh,
        in_specs=(P("hr", None, "st"), P("hr", None, "st"), P(), P(None, "st")),
        out_specs=(P("hr", None, "st"), P(None, "st")),
        check_vma=False,
    )
```

```python
import math

import jax
import jax.numpy as jnp
from jax import lax
from jax.experimental import pallas as pl
from jax.experimental.pallas import tpu as pltpu
from jax.sharding import PartitionSpec as P

F32 = jnp.float32
BF16 = jnp.bfloat16
MESH = pl.DeviceIdType.MESH
LOG2E = 1.0 / math.log(2.0)


def contract(a, b, dim_a, dim_b):
    return lax.dot_general(a, b, (((dim_a,), (dim_b,)), ((), ())), preferred_element_type=F32)


def split3(v):
    high = v.astype(BF16)
    rest = v - high.astype(F32)
    mid = rest.astype(BF16)
    low = (rest - mid.astype(F32)).astype(BF16)
    return high, mid, low


def one_hot_matrix(keep):
    row = lax.broadcasted_iota(jnp.int32, (256, 256), 0)
    col = lax.broadcasted_iota(jnp.int32, (256, 256), 1)
    return jnp.where(keep(row, col), 1.0, 0.0).astype(BF16)


def swap_rows():
    return one_hot_matrix(lambda r, c: ((r >> 4) == (c & 15)) & ((r & 15) == (c >> 4)))


def identity():
    return one_hot_matrix(lambda r, c: r == c)


def swap_leading(src, dst, perm):
    n_a, n_b, width = src.shape
    for b in range(0, n_b, 16):
        for a in range(0, n_a, 16):
            tile = src[a : a + 16, b : b + 16, :].reshape(256, width)
            moved = contract(perm, tile, 1, 0).astype(BF16)
            dst[b : b + 16, a : a + 16, :] = moved.reshape(16, 16, width)


def norm_rows(sq, left, amp_log2):
    parts = [p.astype(F32) for p in split3(sq * (-LOG2E / 32.0) + amp_log2)]
    row = lax.broadcasted_iota(jnp.int32, (16, sq.shape[1]), 0)
    own = 0 if left else 3
    ones = 3 - own
    out = jnp.where((row >= ones) & (row < ones + 3), 1.0, 0.0)
    for q in range(3):
        out = jnp.where(row == own + q, parts[q], out)
    return out.astype(BF16)


def features(e, left, amp_log2):
    sq = jnp.sum(e * e, axis=0, keepdims=True)
    zero = jnp.zeros(e.shape, BF16)
    if left:
        h, m, l = split3(e * (LOG2E / 16.0))
        rows = [h, h, h, norm_rows(sq, True, amp_log2), m, m, l, zero]
    else:
        h, m, l = split3(e)
        rows = [h, m, l, norm_rows(sq, False, 0.0), h, m, h, zero]
    return jnp.concatenate(rows, axis=0)


def kernel(
    cot, field, temporal_in, embed_in, grad, egrad,
    raw, fraw, temporal, embed, sent, fsent, crecv, pair, tile, left, feat_l, feat_r,
    eall, tmix, osend, orecv, esend, erecv, gsend, grecv, inner, cross,
    in_sem, send_sem, recv_sem,
):
    st = lax.axis_index("st")
    hr = lax.axis_index("hr")
    core = lax.rem(st, 2)
    col = st // 2
    me = hr * 8 + col
    x, z, y = st // 4, (hr // 4) * 2 + lax.rem(col, 2), lax.rem(hr, 4)
    partner = (st + 1 - 2 * core, hr)

    def peer(k):
        step = lax.rem(k, 4)
        px = lax.rem(x + step, 4)
        py = lax.rem(y + k // 4 + step, 4)
        pz = lax.rem(z + k // 16 + step, 4)
        return px * 2 + lax.rem(pz, 2), (pz // 2) * 4 + py

    def load(i, src, dst):
        return pltpu.make_async_copy(src, dst, in_sem.at[i])

    load(2, embed_in, embed).start()
    load(0, cot, raw).start()
    load(3, temporal_in, temporal).start()
    load(1, field, fraw).start()

    barrier = pltpu.get_barrier_semaphore()

    @pl.loop(1, 64)
    def _(k):
        c, h = peer(k)
        pl.semaphore_signal(barrier, inc=1, device_id=(c * 2 + core, h), device_id_type=MESH)

    @pl.loop(0, 8)
    def _(c):
        pl.semaphore_signal(barrier, inc=1, device_id=(c * 2 + 1 - core, hr), device_id_type=MESH)

    perm = swap_rows()
    load(0, cot, raw).wait()
    swap_leading(raw, sent, perm)
    load(2, embed_in, embed).wait()
    pl.semaphore_wait(barrier, 71)

    def push(i, src, dst, device):
        pltpu.make_async_remote_copy(
            src_ref=src, dst_ref=dst, send_sem=send_sem.at[i], recv_sem=recv_sem.at[i],
            device_id=device, device_id_type=MESH,
        ).start()

    def keep(i, src, dst):
        pltpu.make_async_copy(src, dst, recv_sem.at[i]).start()

    def settle(sem, ref):
        pltpu.make_async_copy(ref, ref, sem).wait()

    @pl.loop(1, 8)
    def _(k):
        c = lax.rem(col + k, 8)
        push(0, embed, eall.at[0, col], (c * 2 + core, hr))

    keep(0, embed, eall.at[0, col])

    @pl.loop(1, 64)
    def _(k):
        c, h = peer(k)
        push(1, sent.at[h * 8 + c], crecv.at[col, hr], (c * 2 + core, h))

    keep(1, sent.at[me], crecv.at[col, hr])

    load(1, field, fraw).wait()
    swap_leading(fraw, fsent, perm)
    hours = pl.ds(pl.multiple_of(256 + hr * 32, 32), 32)

    def push_field(k):
        c, h = peer(k)
        push(2, fsent.at[h * 8 + c], pair.at[0, col, hours, :], (c * 2 + core, h))

    eye = identity()
    load(3, temporal_in, temporal).wait()
    tmix[...] = contract(eye, temporal[...], 1, 1).astype(BF16)
    amp_log2 = -0.5 * math.log2(4096.0)
    settle(recv_sem.at[0], eall.at[0])
    push(8, eall.at[0], eall.at[1], partner)

    @pl.loop(0, 8, step=2)
    def _(a):
        for q in range(2):
            e = eall[0, a + q]
            feat_l[a + q] = contract(eye, features(e, True, amp_log2), 1, 1).astype(BF16)
            feat_r[0, a + q] = features(e, False, 0.0)

    def station_tiles(a, p):
        rows = feat_l[a]
        for b in range(8):
            tile[a, p, b] = jnp.exp2(contract(rows, feat_r[p, b], 1, 0)).astype(BF16)

    @pl.loop(0, 8)
    def _(a):
        @pl.when(a > 0)
        def _():
            push_field(a * 4)

        for q in range(1, 4):
            push_field(a * 4 + q)
        station_tiles(a, 0)

    settle(recv_sem.at[8], eall.at[1])

    @pl.loop(0, 8, step=2)
    def _(a):
        for q in range(2):
            feat_r[1, a + q] = features(eall[1, a + q], False, 0.0)

    @pl.loop(0, 8)
    def _(a):
        for q in range(4):
            push_field(32 + a * 4 + q)
        station_tiles(a, 1)

    keep(2, fsent.at[me], pair.at[0, col, hours, :])

    settle(recv_sem.at[1], crecv)

    @pl.loop(0, 8, step=2)
    def _(a):
        for q in range(2):
            mixed = contract(tmix[...], crecv[a + q].reshape(256, 256), 1, 0).astype(BF16)
            pair[0, a + q, :256, :] = mixed
        both = pl.ds(a, 2)
        push(3, pair.at[0, both, pl.ds(0, 256), :], pair.at[1, both, pl.ds(0, 256), :], partner)

    @pl.loop(0, 8)
    def _(a):
        left[a, :, 256:] = contract(eye, pair[0, a, :256, :], 1, 1).astype(BF16)

    settle(recv_sem.at[3], pair.at[1, :, pl.ds(0, 256), :])

    def column(k):
        return lax.rem(x + lax.rem(k, 4), 4) * 2 + lax.rem(lax.rem(col, 2) + k // 4, 2)

    def row(k):
        return lax.rem(hr // 4 + k // 4, 2) * 4 + lax.rem(y + k, 4)

    def grad_block(a):
        acc = jnp.zeros((256, 256), F32)
        for p in range(2):
            for b in range(8):
                acc += contract(pair[p, b, :256, :], tile[a, p, b], 1, 1)
        osend[a] = acc.astype(BF16).reshape(8, 32, 256)

    def push_grad(a, first):
        for q in range(first, 8):
            h = row(q)
            push(4, osend.at[a, h], orecv.at[me], (a * 2 + core, h))

    @pl.loop(1, 7, step=2)
    def _(k):
        grad_block(column(k))
        grad_block(column(k + 1))
        push_grad(column(k), 0)
        push_grad(column(k + 1), 0)

    grad_block(column(7))
    grad_block(col)
    push_grad(column(7), 0)
    push_grad(col, 1)
    keep(4, osend.at[col, hr], orecv.at[me])

    settle(recv_sem.at[2], pair.at[0, :, pl.ds(256, 256), :])
    push(5, pair.at[0, :, pl.ds(256, 256), :], pair.at[1, :, pl.ds(256, 256), :], partner)

    @pl.loop(0, 8, step=4)
    def _(first):
        for q in range(4):
            a = first + q
            left[a, :, :256] = pair[0, a, 256:, :].T
            rows = left[a]
            for d in range(5):
                b = lax.rem(a + d, 8)
                gram = contract(rows, pair[0, b], 1, 0).astype(BF16)
                inner[a, d] = gram * tile[a, 0, b]

    settle(recv_sem.at[5], pair.at[1, :, pl.ds(256, 256), :])

    @pl.loop(0, 8, step=4)
    def _(first):
        for q in range(4):
            a = first + q
            rows = left[a]
            for d in range(4):
                b = lax.rem(a + core + d, 8)
                gram = contract(rows, pair[1, b], 1, 0).astype(BF16)
                cross[a, d] = gram * tile[a, 1, b]

    def fold(acc, e):
        return acc[:16] + acc[16:32] + acc[32:48] - e * acc[48:49]

    def other_part(b):
        acc = jnp.zeros((64, 256), F32)
        for d in range(4):
            a = lax.rem(b + 16 - core - d, 8)
            acc += contract(feat_r[0, a, :64, :], cross[a, d], 1, 0)
        return fold(acc, eall[1, b]).astype(BF16)

    def own_part(a):
        acc = jnp.zeros((64, 256), F32)
        for d in range(5):
            acc += contract(feat_r[0, lax.rem(a + d, 8), :64, :], inner[a, d], 1, 1)
        for d in range(4):
            acc += contract(feat_r[1, lax.rem(a + core + d, 8), :64, :], cross[a, d], 1, 1)
        for d in range(1, 4):
            b = lax.rem(a + 8 - d, 8)
            acc += contract(feat_r[0, b, :64, :], inner[b, d], 1, 0)
        return fold(acc, eall[0, a]).astype(BF16)

    @pl.loop(1, 9, step=4)
    def _(k):
        for q in range(4):
            b = lax.rem(col + k + q, 8)
            esend[1, b] = other_part(b)
        for q in range(4):
            b = lax.rem(col + k + q, 8)
            push(6, esend.at[1, b], erecv.at[st], (b * 2 + 1 - core, hr))

    @pl.loop(1, 9, step=2)
    def _(k):
        for q in range(2):
            a = lax.rem(col + k + q, 8)
            esend[0, a] = own_part(a)
        for q in range(2):
            a = lax.rem(col + k + q, 8)

            @pl.when(k + q < 8)
            def _():
                push(6, esend.at[0, a], erecv.at[st], (a * 2 + core, hr))

    erecv[st] = esend[0, col]
    settle(recv_sem.at[6], erecv.at[pl.ds(0, 15)])
    gsend[...] = jnp.sum(erecv[...].astype(F32), axis=0) * (1.0 / 16.0)
    for k in range(1, 8):
        push(7, gsend, grecv.at[hr], (st, lax.rem(hr + k, 8)))
    grecv[hr] = gsend[...]

    settle(recv_sem.at[4], orecv)
    swap_leading(orecv, grad, perm)
    settle(recv_sem.at[7], grecv.at[pl.ds(0, 7)])
    egrad[...] = jnp.sum(grecv[...], axis=0)

    settle(send_sem.at[0], eall.at[0, pl.ds(0, 7)])
    settle(send_sem.at[8], eall.at[1])
    settle(send_sem.at[1], sent.at[pl.ds(0, 63)])
    settle(send_sem.at[2], sent.at[pl.ds(0, 63)])
    settle(send_sem.at[3], pair.at[1, :, pl.ds(0, 256), :])
    settle(send_sem.at[4], orecv.at[pl.ds(0, 63)])
    settle(send_sem.at[5], pair.at[1, :, pl.ds(256, 256), :])
    settle(send_sem.at[6], erecv.at[pl.ds(0, 15)])
    settle(send_sem.at[7], grecv.at[pl.ds(0, 7)])


def on_device(cot, field, temporal, embed):
    hbm = pl.BlockSpec(memory_space=pltpu.HBM)
    vmem = pl.BlockSpec(memory_space=pltpu.VMEM)
    block = (64, 32, 256)
    return pl.pallas_call(
        kernel,
        out_shape=(
            jax.ShapeDtypeStruct((32, 64, 256), BF16),
            jax.ShapeDtypeStruct((16, 256), F32),
        ),
        in_specs=[hbm, hbm, hbm, hbm],
        out_specs=(vmem, vmem),
        scratch_shapes=[
            pltpu.VMEM((32, 64, 256), BF16),
            pltpu.VMEM((32, 64, 256), BF16),
            pltpu.VMEM((256, 256), BF16),
            pltpu.VMEM((16, 256), F32),
            pltpu.VMEM(block, BF16),
            pltpu.VMEM(block, BF16),
            pltpu.VMEM((8, 8, 32, 256), BF16),
            pltpu.VMEM((2, 8, 512, 256), BF16),
            pltpu.VMEM((8, 2, 8, 256, 256), BF16),
            pltpu.VMEM((8, 256, 512), BF16),
            pltpu.VMEM((8, 256, 128), BF16),
            pltpu.VMEM((2, 8, 128, 256), BF16),
            pltpu.VMEM((2, 8, 16, 256), F32),
            pltpu.VMEM((256, 256), BF16),
            pltpu.VMEM((8, 8, 32, 256), BF16),
            pltpu.VMEM(block, BF16),
            pltpu.VMEM((2, 8, 16, 256), BF16),
            pltpu.VMEM((16, 16, 256), BF16),
            pltpu.VMEM((16, 256), F32),
            pltpu.VMEM((8, 16, 256), F32),
            pltpu.VMEM((8, 5, 256, 256), BF16),
            pltpu.VMEM((8, 4, 256, 256), BF16),
            pltpu.SemaphoreType.DMA((4,)),
            pltpu.SemaphoreType.DMA((9,)),
            pltpu.SemaphoreType.DMA((9,)),
        ],
        compiler_params=pltpu.CompilerParams(
            collective_id=0, has_side_effects=True, vmem_limit_bytes=52 * 2**20
        ),
    )(cot, field, temporal, embed)


def solution(mesh):
    return jax.shard_map(
        on_device,
        mesh=mesh,
        in_specs=(P("hr", None, "st"), P("hr", None, "st"), P(), P(None, "st")),
        out_specs=(P("hr", None, "st"), P(None, "st")),
        check_vma=False,
    )
```
